32 devices in a mesh: dp: 4 (over y, x), tensor: 4 (over z), section: 2 (over core).
Axes of the slice: x: 2, y: 2, z: 4, core: 2. Of those that a mesh axis runs over, the one named last changes fastest.
Arguments:
- tokens: bfloat16 [8, 2, 512, 768], P('dp', None, 'tensor'), may hold values from -6 to 6
- cotangent: bfloat16 [8, 2, 512, 768], P('dp', None, 'tensor'), may hold values from -6 to 6
- document_starts: int32 [8, 2, 4], P('dp'), may hold values from 0 to 511, as said below
- valid_count: int32 [8, 2], P('dp'), may hold values from 448 to 512
- reset_flags: int32 [8, 1], P('dp'), may hold values 0 or 1
- memory_init: float32 [16, 768], P('tensor', ('dp', 'section')), may hold values from -6 to 6
- attention_in: float32 [2, 768, 3, 768], P('section', 'dp', None, 'tensor'), may hold values from -0.21875 to 0.21875
- attention_out: float32 [2, 768, 768], P('section', 'tensor', 'dp'), may hold values from -2.5 to 2.5
- feed_expand: float32 [2, 768, 3072], P('section', 'dp', 'tensor'), may hold values from -0.21875 to 0.21875
- feed_reduce: float32 [2, 3072, 768], P('section', 'tensor', 'dp'), may hold values from -0.109375 to 0.109375
- norm_gains: float32 [2, 2, 768], P('section', None, 'dp'), may hold values from 0.4 to 1.6
- norm_shifts: float32 [2, 2, 768], P('section', None, 'dp'), may hold values from -1.8 to 1.8
Outputs:
- layer_ends: bfloat16 [2, 8, 2, 512, 768], P('section', 'dp', None, 'tensor')
- memory_grad: float32 [16, 768], P('tensor', ('dp', 'section'))
- attention_in_grad: float32 [2, 768, 3, 768], P('section', 'dp', None, 'tensor')
- attention_out_grad: float32 [2, 768, 768], P('section', 'tensor', 'dp')
- feed_expand_grad: float32 [2, 768, 3072], P('section', 'dp', 'tensor')
- feed_reduce_grad: float32 [2, 3072, 768], P('section', 'tensor', 'dp')
- norm_gains_grad: float32 [2, 2, 768], P('section', None, 'dp')
- norm_shifts_grad: float32 [2, 2, 768], P('section', None, 'dp')
The draws below stay inside these ranges and needn't reach their ends.
Inputs may be any that keep to these rules, and one draw needn't show every extreme that they name: `document_starts`: each segment's 4 starts increase strictly; the first is 0 and all lie below 512; a document runs from its start to the next start, the last to the segment's end.
All inputs are finite; a program needn't handle non-finite values. No bound on the sum of `reset_flags` on one device may be relied on, other than what follows from the above.
Results may differ from the reference program's by a relative error of at most 0.04.
Values may be sent and summed in bfloat16 or wider, within the bound.
No kernel may reach another device: no remote copies, remote signals or barrier semaphores. Data moves between devices by JAX's collectives and lax.ppermute only.
A program may use at most 192 MiB of HBM per device.

```python
import jax
import jax.numpy as jnp
from jax import lax

D = 768
HEADS = 12
HEAD = 64
FF = 3072
SEG = 512
MEM = 16
SEGS = 2
SEQS = 8
N_TENSOR = 4


def draw_document_starts(key, part):
    key = jax.random.fold_in(key, 7)
    first_key, long_key, last_key = jax.random.split(key, 3)
    pick_key = jax.random.fold_in(key, 11)
    grid_shape = (SEQS, SEGS)
    reach_top = SEG // 8 + 1
    first_end = jax.random.randint(first_key, grid_shape, 1, reach_top)
    long_end = SEG - jax.random.randint(long_key, grid_shape, 2, reach_top)
    room_left = SEG - long_end - 1
    offset_draw = jax.random.randint(last_key, grid_shape, 0, 1 << 20) % room_left
    last_start = long_end + 1 + offset_draw
    picked = jax.random.randint(pick_key, (), 0, SEQS * SEGS)
    flat_place = jnp.arange(SEQS * SEGS).reshape(grid_shape)
    last_start = jnp.where(flat_place == picked, SEG - 1, last_start)
    zero_col = jnp.zeros(grid_shape, jnp.int32)
    return jnp.stack([zero_col, first_end, long_end, last_start], -1).astype(jnp.int32)


def touch_ends(result, key, low, high):
    index_at = [jax.random.randint(jax.random.fold_in(key, axis), (), 0, length) for axis, length in enumerate(result.shape)]
    widest = result.shape.index(max(result.shape))
    neighbour = index_at[:widest] + [(index_at[widest] + 1) % result.shape[widest]] + index_at[widest + 1:]
    return result.at[tuple(index_at)].set(low).at[tuple(neighbour)].set(high)


def spiked(drawn, rng, source, target, shards_of, factor):
    def block_of(dim):
        return (jnp.arange(drawn.shape[dim]) // (drawn.shape[dim] // shards_of)).reshape((-1,) + (1,) * (drawn.ndim - 1 - dim))

    first = jax.random.permutation(rng, shards_of)[block_of(target)]
    far = (block_of(target) + shards_of // 2) % shards_of
    return jnp.where((block_of(source) == first) | (block_of(source) == far), factor * drawn, drawn)


def level_of(rng, shape, pieces, low, top_value):
    loudness, own = 1.0, jax.random.fold_in(rng, 6)
    for position, parts in pieces:
        steps = jnp.exp(jax.random.uniform(jax.random.fold_in(own, position), (parts,), jnp.float32, low / len(pieces), top_value / len(pieces)))
        loudness = loudness * jnp.repeat(steps, shape[position] // parts).reshape([-1 if axis == position else 1 for axis in range(len(shape))])
    return loudness


def scatter_about(own_key, shape, deviation, limit, pieces=(), held_as=jnp.bfloat16):
    factor_of = level_of(own_key, shape, pieces, -0.22, 0.18) if pieces else 1.0
    array = jax.random.normal(own_key, shape, jnp.float32) * deviation * factor_of
    return jnp.minimum(jnp.maximum(array, -limit), limit).astype(held_as)


def noise_with(own_key, extent, deviation, bound, shards, heavy, held_as=jnp.bfloat16):
    values = deviation * jax.random.normal(own_key, extent, jnp.float32)
    if shards:
        values = values * level_of(own_key, extent, shards, -0.22, 0.18)
    return jnp.clip(spiked(values, jax.random.fold_in(own_key, 3), *heavy), -bound, bound).astype(held_as)


def setup_inputs(seed: int = 0) -> dict:
    keys = jax.random.split(jax.random.key(seed), 13)
    return {
        "tokens": scatter_about(keys[0], (SEQS, SEGS, SEG, D), 1.0, 6.0, ((0, 4), (2, 4))),
        "cotangent": noise_with(keys[1], (SEQS, SEGS, SEG, D), 1.0, 6.0, ((0, 4), (2, 4)), (0, 3, 4, 2.0)),
        "document_starts": draw_document_starts(jax.random.fold_in(keys[12], 71), 0),
        "valid_count": touch_ends(jax.random.randint(keys[3], (SEQS, SEGS), SEG - SEG // 8, SEG + 1), jax.random.fold_in(keys[3], 1), SEG - SEG // 8, SEG).astype(jnp.int32),
        "reset_flags": touch_ends((jax.random.randint(keys[4], (SEQS, SEGS - 1), 0, 4) < 1).astype(jnp.int32), jax.random.fold_in(keys[4], 1), 0, 1),
        "memory_init": scatter_about(keys[5], (MEM, D), 1.0, 6.0, ((0, 4), (1, 8)), jnp.float32),
        "attention_in": scatter_about(keys[6], (2, D, 3, D), D ** -0.5, 0.21875, ((0, 2), (1, 4), (3, 4)), jnp.float32),
        "attention_out": scatter_about(keys[7], (2, D, D), (max(D // 128, 1)) ** -0.5, 2.5, ((0, 2), (1, 4), (2, 4)), jnp.float32),
        "feed_expand": scatter_about(keys[8], (2, D, FF), D ** -0.5, 0.21875, ((0, 2), (1, 4), (2, 4)), jnp.float32),
        "feed_reduce": scatter_about(keys[9], (2, FF, D), FF ** -0.5, 0.109375, ((0, 2), (1, 4), (2, 4)), jnp.float32),
        "norm_gains": jnp.clip(1.0 + 0.12 * jax.random.normal(keys[10], (2, 2, D), jnp.float32), 0.4, 1.6),
        "norm_shifts": scatter_about(keys[11], (2, 2, D), 0.3, 1.8, ((0, 2), (2, 4)), jnp.float32),
    }


@jax.custom_vjp
def low(v):
    return lax.optimization_barrier(v.astype(jnp.bfloat16)).astype(jnp.float32)

@jax.custom_vjp
def low_back(v):
    return v

def low_keep(v):
    return (low(v), None)

def low_pass(kept, grad):
    return (grad,)

def back_keep(v):
    return (v, None)

def back_low(kept, grad):
    return (low(grad),)
low.defvjp(low_keep, low_pass)
low_back.defvjp(back_keep, back_low)

def norm_rows(values, gain_row, shift_row):
    mean_row = lax.optimization_barrier(jnp.mean(values, -1, keepdims=True))
    centred = values - mean_row
    spread = lax.optimization_barrier(jnp.mean(centred * centred, -1, keepdims=True))
    return centred * lax.rsqrt(spread + 1e-05) * gain_row + shift_row

def gelu_exact(values):
    return 0.5 * values * (1.0 + lax.erf(values * 0.7071067811865476))

def allowed_natural(starts, valid):
    row_place = jnp.arange(MEM + SEG)
    is_memory = row_place < MEM
    token_index = row_place - MEM
    doc_index = lax.optimization_barrier(jnp.sum((starts[None, :] <= token_index[:, None]).astype(jnp.int32), -1))
    key_live = is_memory | (token_index < valid)
    same_doc = doc_index[:, None] == doc_index[None, :]
    return key_live[None, :] & (is_memory[:, None] | is_memory[None, :] | same_doc)

def layer(row_block, allowed, inputs_weight, outputs_weight, expand_weight, reduce_weight, gain_rows, shift_rows):
    span_cols = D // N_TENSOR
    heads_local = HEADS // N_TENSOR
    wide_cols = FF // N_TENSOR
    total_rows = row_block.shape[0]
    scale = HEAD ** (-0.5)
    highest = lax.Precision.HIGHEST
    attn_sum = jnp.zeros_like(row_block)
    for group in range(N_TENSOR):
        projected = jnp.einsum('rd,dkc->rkc', row_block, inputs_weight[:, :, group * span_cols:(group + 1) * span_cols], precision=highest)
        projected = low(low_back(projected)).reshape(total_rows, 3, heads_local, HEAD)
        queries = projected[:, 0]
        key_rows = projected[:, 1]
        value_rows = projected[:, 2]
        scores = low_back(jnp.einsum('qhe,khe->hqk', queries, key_rows, precision=highest) * scale)
        scores = jnp.where(allowed[None], scores, -1000000000.0)
        top_score = lax.optimization_barrier(jnp.max(scores, -1, keepdims=True))
        exp_scores = jnp.exp(scores - top_score)
        probs = low(exp_scores / lax.optimization_barrier(jnp.sum(exp_scores, -1, keepdims=True)))
        mixed = jnp.einsum('hqk,khe->qhe', probs, value_rows, precision=highest)
        mixed = low(low_back(mixed)).reshape(total_rows, span_cols)
        attn_sum = attn_sum + jnp.dot(mixed, outputs_weight[group * span_cols:(group + 1) * span_cols], precision=highest)
    attn_sum = low_back(attn_sum)
    normed = norm_rows(row_block + attn_sum, gain_rows[0], shift_rows[0])
    normed_low = low(normed)
    ffn_sum = jnp.zeros_like(row_block)
    for group in range(N_TENSOR):
        hidden = low_back(jnp.dot(normed_low, expand_weight[:, group * wide_cols:(group + 1) * wide_cols], precision=highest))
        active = low(gelu_exact(hidden))
        ffn_sum = ffn_sum + jnp.dot(active, reduce_weight[group * wide_cols:(group + 1) * wide_cols], precision=highest)
    ffn_sum = low_back(ffn_sum)
    return low(low_back(norm_rows(normed + ffn_sum, gain_rows[1], shift_rows[1])))

def sequence_forward(param_set, token_values, starts, valid, resets):
    memory_init, attention_in, attention_out, feed_expand, feed_reduce, norm_gains, norm_shifts = param_set
    init_rows = low(memory_init)
    inputs_weight = low(attention_in)
    outputs_weight = low(attention_out)
    expand_weight = low(feed_expand)
    reduce_weight = low(feed_reduce)
    gain_rows = low(norm_gains)
    shift_rows = low(norm_shifts)
    memory_rows = init_rows
    results = []
    for segment in range(SEGS):
        if segment > 0:
            memory_rows = jnp.where(resets[segment - 1] > 0, init_rows, memory_rows)
        row_block = low_back(jnp.concatenate([memory_rows, token_values[segment]], 0))
        allowed = allowed_natural(starts[segment], valid[segment])
        for depth in range(2):
            row_block = layer(row_block, allowed, inputs_weight[depth], outputs_weight[depth], expand_weight[depth], reduce_weight[depth], gain_rows[depth], shift_rows[depth])
        memory_rows = row_block[:MEM]
        results.append(row_block[MEM:])
    return jnp.stack(results)

def reference(tokens, cotangent, document_starts, valid_count, reset_flags, memory_init, attention_in, attention_out, feed_expand, feed_reduce, norm_gains, norm_shifts):
    params = (memory_init, attention_in, attention_out, feed_expand, feed_reduce, norm_gains, norm_shifts)
    token_place = jnp.arange(SEG)

    def per_sequence(grad_sums, seq_inputs):
        seq_tokens, seq_cot, seq_starts, seq_valid, seq_reset = seq_inputs
        live_rows = (token_place[None, :] < seq_valid[:, None])[:, :, None]
        seq_cot = jnp.where(live_rows, seq_cot.astype(jnp.float32), jnp.zeros_like(seq_cot, dtype=jnp.float32))

        def forward(param_set, token_values):
            return sequence_forward(param_set, token_values, seq_starts, seq_valid, seq_reset)
        outputs, pull = jax.vjp(forward, params, seq_tokens.astype(jnp.float32))
        param_grads, token_grads = pull(seq_cot)
        grad_sums = jax.tree.map(jnp.add, grad_sums, param_grads)
        return (grad_sums, (outputs.astype(jnp.bfloat16), token_grads.astype(jnp.bfloat16)))
    zero_sums = tuple((jnp.zeros(param.shape, jnp.float32) for param in params))
    grad_sums, (all_outputs, all_token_grads) = lax.scan(per_sequence, zero_sums, (tokens, cotangent, document_starts, valid_count, reset_flags))
    layer_ends = jnp.stack([all_token_grads, all_outputs], 0)
    return (layer_ends, grad_sums[0], grad_sums[1], grad_sums[2], grad_sums[3], grad_sums[4], grad_sums[5], grad_sums[6])
```

```python
import functools

import jax
import jax.numpy as jnp
from jax import lax
from jax.experimental import pallas as pl
from jax.experimental.pallas import tpu as pltpu
from jax.sharding import PartitionSpec as P

HEAD = 64
LOW = jnp.bfloat16
WIDE = jnp.float32
PAIR = 2 * HEAD


def swap(block, axis, mask):
    return lax.ppermute(block, axis, [(i, i ^ mask) for i in range(lax.axis_size(axis))])


def route(block, pairs_of):
    tensor_count, section_count = (lax.axis_size("tensor"), lax.axis_size("section"))
    pairs = []
    for t in range(tensor_count):
        for s in range(section_count):
            to = pairs_of(t, s)
            if to is not None:
                pairs.append((t * section_count + s, to[0] * section_count + to[1]))
    return lax.ppermute(block, ("tensor", "section"), pairs)


def dot(left, right, contract):
    return lax.dot_general(left, right, (contract, ((), ())), preferred_element_type=WIDE)


def nn(left, right):
    return dot(left, right, ((1,), (0,)))


def nt(left, right):
    return dot(left, right, ((1,), (1,)))


def tn(left, right):
    return dot(left, right, ((0,), (0,)))


def bits_of(count):
    return count.bit_length() - 1


def own_order(values):
    count = lax.axis_size("dp")
    place = lax.axis_index("dp")
    width = values.shape[-1]
    lead = values.shape[:-1]
    for bit in range(bits_of(count)):
        step = 1 << bit
        cut = values.reshape(lead + (count // (2 * step), 2, width * step // count))
        turned = jnp.concatenate([cut[..., 1:2, :], cut[..., 0:1, :]], -2).reshape(values.shape)
        values = jnp.where((place >> bit) & 1 == 1, turned, values)
    return values


def gather_pair(first, second):
    for mask in (2, 1):
        width = first.shape[1]
        came = swap(jnp.concatenate([first, second], 1), "tensor", mask)
        first = jnp.concatenate([first, came[:, :width]], 1)
        second = jnp.concatenate([second, came[:, width:]], 1)
    count = bits_of(lax.axis_size("dp"))
    rows, width = first.shape
    first = first.reshape((1,) * count + first.shape)
    second = second.reshape((1,) * count + second.shape)
    for step in range(count):
        low, high = (step, count - 1 - step)
        came_first = swap(first, "dp", 1 << low)
        came_second = swap(second, "dp", 1 << high)
        first = jnp.concatenate([first, came_first], count - 1 - low)
        second = jnp.concatenate([second, came_second], count - 1 - high)
    full = (rows << count, width)
    return (first.reshape(full), second.reshape(full))


def scatter_pair(first, second):
    count = bits_of(lax.axis_size("dp"))
    rows, width = first.shape
    cut = (2,) * count + (rows >> count, width)
    first = first.reshape(cut)
    second = second.reshape(cut)

    def halves(block, axis):
        return (lax.slice_in_dim(block, 0, 1, axis=axis), lax.slice_in_dim(block, 1, 2, axis=axis))

    for step in range(count):
        high, low = (count - 1 - step, step)
        keep_first, send_first = halves(first, count - 1 - high)
        keep_second, send_second = halves(second, count - 1 - low)
        came_first = swap(send_first, "dp", 1 << high)
        came_second = swap(send_second, "dp", 1 << low)
        first = add_low(keep_first, came_first)
        second = add_low(keep_second, came_second)
    first = first.reshape(rows >> count, width)
    second = second.reshape(rows >> count, width)
    for mask in (1, 2):
        half = first.shape[1] // 2
        came = swap(jnp.concatenate([first[:, half:], second[:, half:]], 1), "tensor", mask)
        first = add_low(first[:, :half], came[:, :half])
        second = add_low(second[:, :half], came[:, half:])
    return (first, second)


def add_low(left, right):
    return (left.astype(WIDE) + right.astype(WIDE)).astype(LOW)


def norm_forward(values, gain, shift):
    centred = values - jnp.mean(values, -1, keepdims=True)
    scale = lax.rsqrt(jnp.mean(centred * centred, -1, keepdims=True) + 1e-05)
    plain = centred * scale
    return (plain * gain + shift, plain, scale)


def norm_backward(grad, plain, scale, gain):
    inner = grad * gain
    mean_inner = jnp.mean(inner, -1, keepdims=True)
    mean_along = jnp.mean(inner * plain, -1, keepdims=True)
    return (
        scale * (inner - mean_inner - plain * mean_along),
        jnp.sum(grad * plain, 0),
        jnp.sum(grad, 0),
    )


def attention_kernel(q_ref, k_ref, v_ref, allowed_ref, mixed_ref, mass_ref):
    queries, keys, values = (q_ref[...], k_ref[...], v_ref[...])
    allowed = allowed_ref[...] > 0
    lower = lax.broadcasted_iota(jnp.int32, queries.shape, 1) < HEAD
    mixed, mass = ([], [])
    for side in (lower, ~lower):
        scores = nt(jnp.where(side, queries, jnp.zeros_like(queries)), keys) * HEAD ** (-0.5)
        scores = jnp.where(allowed, scores, -1e9)
        top = jnp.max(scores, -1, keepdims=True)
        raised = jnp.exp(scores - top)
        total = jnp.sum(raised, -1, keepdims=True)
        mixed.append(nn((raised / total).astype(LOW), values))
        mass.append(top + jnp.log(total))
    mixed_ref[...] = jnp.where(lower, mixed[0], mixed[1]).astype(LOW)
    mass_ref[...] = jnp.where(lower, mass[0], mass[1])


def attention_back_kernel(
    q_ref, k_ref, v_ref, allowed_ref, grad_ref, mass_ref, gq_ref, gk_ref, gv_ref
):
    queries, keys, values, grad = (q_ref[...], k_ref[...], v_ref[...], grad_ref[...])
    allowed = allowed_ref[...] > 0
    mass = mass_ref[...]
    lower = lax.broadcasted_iota(jnp.int32, queries.shape, 1) < HEAD
    lower_keys = lax.broadcasted_iota(jnp.int32, keys.shape, 1) < HEAD
    scale = HEAD ** (-0.5)
    none = jnp.zeros_like(queries)
    grad_q, grad_k, grad_v = ([], [], [])
    for side, column in ((lower, 0), (~lower, HEAD)):
        scores = nt(jnp.where(side, queries, none), keys) * scale
        probs = jnp.where(allowed, jnp.exp(scores - mass[:, column : column + 1]), 0.0)
        grad_probs = nt(jnp.where(side, grad, none), values)
        inner = jnp.sum(probs * grad_probs, -1, keepdims=True)
        grad_scores = (probs * (grad_probs - inner)).astype(LOW)
        grad_q.append(nn(grad_scores, keys) * scale)
        grad_k.append(tn(grad_scores, queries) * scale)
        grad_v.append(tn(probs.astype(LOW), grad))
    gq_ref[...] = jnp.where(lower, grad_q[0], grad_q[1]).astype(LOW)
    gk_ref[...] = jnp.where(lower_keys, grad_k[0], grad_k[1]).astype(LOW)
    gv_ref[...] = jnp.where(lower_keys, grad_v[0], grad_v[1]).astype(LOW)


def attention_specs(rows, keys):
    row_spec = pl.BlockSpec((rows, PAIR), lambda i: (0, i))
    key_spec = pl.BlockSpec((keys, PAIR), lambda i: (0, i))
    allowed_spec = pl.BlockSpec((rows, keys), lambda i: (0, 0))
    return (row_spec, key_spec, allowed_spec)


def attention(queries, keys, values, allowed):
    rows, width = queries.shape
    row_spec, key_spec, allowed_spec = attention_specs(rows, keys.shape[0])
    work = 4 * rows * keys.shape[0] * width
    return pl.pallas_call(
        attention_kernel,
        grid=(width // PAIR,),
        in_specs=[row_spec, key_spec, key_spec, allowed_spec],
        out_specs=[row_spec, row_spec],
        out_shape=[
            jax.ShapeDtypeStruct((rows, width), LOW),
            jax.ShapeDtypeStruct((rows, width), WIDE),
        ],
        cost_estimate=pl.CostEstimate(flops=2 * work, bytes_accessed=4000000, transcendentals=0),
    )(queries, keys, values, allowed)


def attention_back(queries, keys, values, allowed, grad, mass):
    rows, width = queries.shape
    row_spec, key_spec, allowed_spec = attention_specs(rows, keys.shape[0])
    work = 10 * rows * keys.shape[0] * width
    return pl.pallas_call(
        attention_back_kernel,
        grid=(width // PAIR,),
        in_specs=[row_spec, key_spec, key_spec, allowed_spec, row_spec, row_spec],
        out_specs=[row_spec, key_spec, key_spec],
        out_shape=[
            jax.ShapeDtypeStruct((rows, width), LOW),
            jax.ShapeDtypeStruct(keys.shape, LOW),
            jax.ShapeDtypeStruct(keys.shape, LOW),
        ],
        cost_estimate=pl.CostEstimate(flops=2 * work, bytes_accessed=6000000, transcendentals=0),
    )(queries, keys, values, allowed, grad, mass)


def layer_forward(rows, key_rows, allowed, weights, gains, shifts):
    (w_q, w_k, w_v, w_out), expand, reduce = weights
    queries = nn(rows, w_q).astype(LOW)
    keys = nn(key_rows, w_k).astype(LOW)
    values = nn(key_rows, w_v).astype(LOW)
    mixed, mass = attention(queries, keys, values, allowed)
    first_sum = rows.astype(WIDE) + nt(mixed, w_out)
    normed, plain_one, scale_one = norm_forward(first_sum, gains[0], shifts[0])
    normed_low = normed.astype(LOW)
    hidden = [nn(normed_low, part) for part in expand]
    active = [
        (0.5 * part * (1.0 + lax.erf(part * 0.7071067811865476))).astype(LOW) for part in hidden
    ]
    second_sum = normed + sum(nt(act, part) for act, part in zip(active, reduce))
    result, plain_two, scale_two = norm_forward(second_sum, gains[1], shifts[1])
    kept = (
        (rows, key_rows, queries, keys, values, mixed, mass, allowed),
        (plain_one, scale_one, normed_low, hidden, active, plain_two, scale_two),
    )
    return (result.astype(LOW), kept)


def layer_backward(grad_out, kept, weights, gains):
    (w_q, w_k, w_v, w_out), expand, reduce = weights
    (rows, key_rows, queries, keys, values, mixed, mass, allowed) = kept[0]
    (plain_one, scale_one, normed_low, hidden, active, plain_two, scale_two) = kept[1]
    grad_second, gain_two, shift_two = norm_backward(
        grad_out.astype(WIDE), plain_two, scale_two, gains[1]
    )
    grad_ffn = grad_second.astype(LOW)
    grad_hidden = []
    for part, hid in zip(reduce, hidden):
        slope = 0.5 * (1.0 + lax.erf(hid * 0.7071067811865476)) + hid * (
            0.3989422804014327 * jnp.exp(-0.5 * hid * hid)
        )
        grad_hidden.append((nn(grad_ffn, part) * slope).astype(LOW))
    grad_normed = grad_second + sum(nt(grad, part) for grad, part in zip(grad_hidden, expand))
    grad_first, gain_one, shift_one = norm_backward(grad_normed, plain_one, scale_one, gains[0])
    grad_attn = grad_first.astype(LOW)
    grad_mixed = nn(grad_attn, w_out).astype(LOW)
    grad_q, grad_k, grad_v = attention_back(queries, keys, values, allowed, grad_mixed, mass)
    key_part = nt(grad_k, w_k) + nt(grad_v, w_v)
    own_part = grad_first + nt(grad_q, w_q)
    terms = (
        (rows, key_rows, grad_q, grad_k, grad_v, mixed, grad_attn),
        (normed_low, grad_hidden, active, grad_ffn),
    )
    norm_terms = jnp.stack([gain_one, gain_two, shift_one, shift_two], 0)
    return (own_part, key_part, terms, norm_terms)


def gather_keys(tokens):
    across = swap(tokens, "tensor", 1)
    return [tokens, swap(tokens, "section", 1), across, swap(across, "section", 1)]


def collect_rows(own_part, key_part, quarter):
    mine = own_part[:quarter] + key_part[:quarter]
    beside = key_part[quarter : 2 * quarter]
    across = key_part[2 * quarter : 3 * quarter]
    far = key_part[3 * quarter : 4 * quarter]
    memory = own_part[quarter:] + key_part[4 * quarter :]
    came = swap(jnp.concatenate([beside, far, memory], 0).astype(LOW), "section", 1).astype(WIDE)
    mine = mine + came[:quarter]
    across = across + came[quarter : 2 * quarter]
    memory = memory + came[2 * quarter :]
    came = swap(jnp.concatenate([across, memory], 0).astype(LOW), "tensor", 1).astype(WIDE)
    return ((mine + came[:quarter]).astype(LOW), (memory + came[quarter:]).astype(LOW))


def shards(
    tokens,
    cotangent,
    document_starts,
    valid_count,
    reset_flags,
    memory_init,
    attention_in,
    attention_out,
    feed_expand,
    feed_reduce,
    norm_gains,
    norm_shifts,
):
    dp_count, tensor_count, section_count = (lax.axis_size(a) for a in ("dp", "tensor", "section"))
    dp_place, tensor_place = (lax.axis_index("dp"), lax.axis_index("tensor"))
    first_section = lax.axis_index("section") == 0
    first_group = tensor_place // 2 == 0
    counts_memory = first_section & (tensor_place % 2 == 0)
    segments, quarter, width = tokens.shape[1:]
    memory_count = memory_init.shape[0] * tensor_count
    block = attention_in.shape[1]
    unit_half = feed_expand.shape[2] // 2

    def by_section(at_first, at_second):
        return jnp.where(first_section, at_first, at_second)

    def of_group(array):
        return jnp.where(first_group, array[0], array[1])

    def of_other(array):
        return jnp.where(first_group, array[1], array[0])

    def quarter_rows(array):
        came = route(of_other(array), lambda t, s: (t ^ 2, 1) if s == 1 else None)
        return own_order(by_section(of_group(array), came))

    token_parts = [gather_keys(quarter_rows(tokens[:, 0]))]

    small = jnp.concatenate(
        [memory_init.reshape(-1), norm_gains.reshape(-1), norm_shifts.reshape(-1)]
    ).astype(LOW)
    small = lax.all_gather(small, ("dp", "tensor", "section"), axis=0, tiled=False)
    small = small.reshape(dp_count, tensor_count, section_count, -1)
    memory_size = memory_init.size
    init_rows = small[..., :memory_size].reshape(
        dp_count, tensor_count, section_count, memory_init.shape[0], memory_init.shape[1]
    )
    init_rows = own_order(init_rows.transpose(1, 3, 0, 2, 4).reshape(memory_count, width))
    norm_rows = small[:, 0, :, memory_size:].reshape(dp_count, section_count, 4, block)
    norm_rows = norm_rows.transpose(1, 2, 0, 3).reshape(section_count, 4, width)
    norm_rows = own_order(norm_rows).astype(WIDE)
    gains = norm_rows[:, 0:2]
    shifts = norm_rows[:, 2:4]

    low_in = attention_in[0].astype(LOW)
    low_out = attention_out[0].astype(LOW).T
    low_expand = feed_expand[0].astype(LOW)
    low_reduce = feed_reduce[0].astype(LOW).T
    halves = (
        jnp.concatenate(
            [low_in[:, 0], low_in[:, 1], low_expand[:, :unit_half], low_reduce[:, :unit_half]], 1
        ),
        jnp.concatenate(
            [low_in[:, 2], low_out, low_expand[:, unit_half:], low_reduce[:, unit_half:]], 1
        ),
    )
    mine = by_section(halves[0], halves[1])
    came = swap(by_section(halves[1], halves[0]), "section", 1)
    layer_shards = (by_section(mine, came), by_section(came, mine))
    cols = low_out.shape[1]
    weights = []
    for shard in layer_shards:
        one, two = gather_pair(shard[:, :cols], shard[:, cols : 2 * cols])
        came_one, came_two = (swap(one, "section", 1), swap(two, "section", 1))
        attention_weights = (
            by_section(one, came_one),
            by_section(two, came_two),
            by_section(came_one, one),
            by_section(came_two, two),
        )
        expand, reduce = gather_pair(
            shard[:, 2 * cols : 2 * cols + unit_half], shard[:, 2 * cols + unit_half :]
        )
        weights.append(
            (
                attention_weights,
                (expand, swap(expand, "section", 1)),
                (reduce, swap(reduce, "section", 1)),
            )
        )

    starts, valid, resets = (of_group(document_starts), of_group(valid_count), of_group(reset_flags))
    for segment in range(1, segments):
        token_parts.append(gather_keys(quarter_rows(tokens[:, segment])))
    grad_ends = [quarter_rows(cotangent[:, segment]) for segment in range(segments)]

    def places(across, beside):
        at = tensor_place ^ across
        at = by_section(at ^ (2 * beside), at ^ (2 * (1 - beside)))
        return at * quarter + jnp.arange(quarter)

    memory_places = jnp.full((memory_count,), -1)
    row_places = jnp.concatenate([places(0, 0), memory_places])
    key_places = jnp.concatenate(
        [places(0, 0), places(0, 1), places(1, 0), places(1, 1), memory_places]
    )

    def allowed_of(segment):
        row_doc = jnp.sum(starts[segment][None, :] <= row_places[:, None], -1)
        key_doc = jnp.sum(starts[segment][None, :] <= key_places[:, None], -1)
        live = key_places < valid[segment]
        either = (row_places < 0)[:, None] | (key_places < 0)[None, :]
        return (live[None, :] & (either | (row_doc[:, None] == key_doc[None, :]))).astype(WIDE)

    kept = []
    ends = []
    memory_rows = init_rows
    for segment in range(segments):
        if segment > 0:
            memory_rows = jnp.where(resets[segment - 1] > 0, init_rows, memory_rows)
        allowed = allowed_of(segment)
        parts = token_parts[segment]
        kept.append([])
        for layer in range(2):
            rows = jnp.concatenate([parts[0], memory_rows], 0)
            key_rows = jnp.concatenate(parts + [memory_rows], 0)
            result, state = layer_forward(
                rows, key_rows, allowed, weights[layer], gains[layer], shifts[layer]
            )
            kept[segment].append(state)
            memory_rows = result[quarter:]
            if layer == 0:
                parts = gather_keys(result[:quarter])
        ends.append(result[:quarter])

    token_grads = [None] * segments
    terms = [[None] * segments for _ in range(2)]
    norm_sums = [0.0, 0.0]
    memory_sum = jnp.zeros((memory_count, width), WIDE)
    memory_grad = jnp.zeros((memory_count, width), LOW)
    for segment in reversed(range(segments)):
        live = places(0, 0) < valid[segment]
        token_grad = jnp.where(live[:, None], grad_ends[segment], jnp.zeros_like(grad_ends[segment]))
        for layer in (1, 0):
            grad_out = jnp.concatenate([token_grad, memory_grad], 0)
            own_part, key_part, terms[layer][segment], norm_terms = layer_backward(
                grad_out, kept[segment][layer], weights[layer], gains[layer]
            )
            norm_sums[layer] = norm_sums[layer] + norm_terms
            token_grad, memory_grad = collect_rows(own_part, key_part, quarter)
            memory_grad = jnp.where(counts_memory, memory_grad, jnp.zeros_like(memory_grad))
        token_grads[segment] = token_grad
        wide_grad = memory_grad.astype(WIDE)
        if segment > 0:
            reset = resets[segment - 1] > 0
            memory_sum = memory_sum + jnp.where(reset, wide_grad, 0.0)
            memory_grad = jnp.where(reset, jnp.zeros_like(memory_grad), memory_grad)
        else:
            memory_sum = memory_sum + wide_grad

    def stacked(layer, which, index):
        return jnp.concatenate([term[which][index] for term in terms[layer]], 0)

    owned = [None, None]
    for layer in (1, 0):
        normed_low = stacked(layer, 1, 0)
        grad_ffn = stacked(layer, 1, 3)
        grad_hidden, active = (
            [jnp.concatenate([term[1][which][half] for term in terms[layer]], 0) for half in (0, 1)]
            for which in (1, 2)
        )
        expand_own, expand_send = (tn(normed_low, part).astype(LOW) for part in grad_hidden)
        reduce_own, reduce_send = (tn(grad_ffn, part).astype(LOW) for part in active)
        expand, reduce = scatter_pair(
            add_low(expand_own, swap(expand_send, "section", 1)),
            add_low(reduce_own, swap(reduce_send, "section", 1)),
        )
        rows, key_rows, grad_q, grad_k, grad_v, mixed, grad_attn = (
            stacked(layer, 0, index) for index in range(7)
        )
        grads = [
            tn(rows, grad_q).astype(LOW),
            tn(key_rows, grad_k).astype(LOW),
            tn(key_rows, grad_v).astype(LOW),
            tn(grad_attn, mixed).astype(LOW),
        ]
        one, two = scatter_pair(
            *(
                add_low(
                    by_section(grads[place], grads[place + 2]),
                    swap(by_section(grads[place + 2], grads[place]), "section", 1),
                )
                for place in (0, 1)
            )
        )
        owned[layer] = jnp.concatenate([one, two, expand, reduce], 1)
    came = swap(by_section(owned[1], owned[0]), "section", 1)
    first_half = by_section(owned[0], came).astype(WIDE)
    second_half = by_section(came, owned[1]).astype(WIDE)

    def cut(array, place):
        if place < 2:
            return array[:, place * cols : (place + 1) * cols]
        start = 2 * cols + (place - 2) * unit_half
        return array[:, start : start + unit_half]

    in_grad = jnp.stack([cut(first_half, 0), cut(first_half, 1), cut(second_half, 0)], 1)[None]
    out_grad = cut(second_half, 1).T[None]
    expand_grad = jnp.concatenate([cut(first_half, 2), cut(second_half, 2)], 1)[None]
    reduce_grad = jnp.concatenate([cut(first_half, 3), cut(second_half, 3)], 1).T[None]

    sums = own_order(jnp.concatenate([memory_sum, norm_sums[0], norm_sums[1]], 0))
    sums = lax.psum(sums, ("dp", "tensor", "section"))
    memory_cols = memory_init.shape[1]
    memory_grad = lax.dynamic_slice(
        sums,
        (
            tensor_place * memory_init.shape[0],
            (dp_place * section_count + lax.axis_index("section")) * memory_cols,
        ),
        memory_init.shape,
    )
    norm_grads = lax.dynamic_slice(
        by_section(sums[memory_count : memory_count + 4], sums[memory_count + 4 :]),
        (0, dp_place * block),
        (4, block),
    )

    outs = jnp.stack(ends, 0)
    grads = jnp.stack(token_grads, 0)
    out_near = route(outs, lambda t, s: (t, 1) if s == 0 else None)
    out_far = route(outs, lambda t, s: (t ^ 2, 1) if s == 1 else None)
    grad_far = route(grads, lambda t, s: (t ^ 2, 0) if s == 1 else None)
    near = by_section(grads, out_near)
    far = by_section(grad_far, out_far)
    layer_ends = own_order(
        jnp.stack([jnp.where(first_group, near, far), jnp.where(first_group, far, near)], 0)
    )[None]
    return (
        layer_ends,
        memory_grad,
        in_grad,
        out_grad,
        expand_grad,
        reduce_grad,
        norm_grads[None, 0:2],
        norm_grads[None, 2:4],
    )


def solution(mesh):
    in_specs = (
        P("dp", None, "tensor", None),
        P("dp", None, "tensor", None),
        P("dp", None, None),
        P("dp", None),
        P("dp", None),
        P("tensor", ("dp", "section")),
        P("section", "dp", None, "tensor"),
        P("section", "tensor", "dp"),
        P("section", "dp", "tensor"),
        P("section", "tensor", "dp"),
        P("section", None, "dp"),
        P("section", None, "dp"),
    )
    out_specs = (
        P("section", "dp", None, "tensor", None),
        P("tensor", ("dp", "section")),
        P("section", "dp", None, "tensor"),
        P("section", "tensor", "dp"),
        P("section", "dp", "tensor"),
        P("section", "tensor", "dp"),
        P("section", None, "dp"),
        P("section", None, "dp"),
    )
    return jax.shard_map(shards, mesh=mesh, in_specs=in_specs, out_specs=out_specs, check_vma=False)
```
